256 devices in a mesh: dp: 64 (over x, z_hi, y), mp: 4 (over z_lo, core).
Axes of the slice: x: 4, y: 4, z: 8 (z_hi: 4, z_lo: 2; z = z_hi * 2 + z_lo), core: 2. Of those that a mesh axis runs over, the one named last changes fastest.
Arguments:
- acts: bfloat16 [49152, 4096], P('dp', 'mp'), may hold values from -64 to 64
- grads: bfloat16 [49152, 4096], P('dp', 'mp'), may hold values from -64 to 64
- kinds: int32 [49152], P('dp'), may hold values from 0 to 2, as said below
- act_basis: bfloat16 [8, 512, 512], P('mp', 'dp'), may hold values from -0.25 to 0.25
- grad_basis: bfloat16 [8, 512, 512], P('mp', 'dp'), may hold values from -0.25 to 0.25
Outputs:
- act_factor: float32 [8, 512, 512], P('mp', 'dp')
- grad_factor: float32 [8, 512, 512], P('mp', 'dp')
- eigenvalues: float32 [4096, 4096], P('dp', 'mp')
The draws below stay inside these ranges and needn't reach their ends.
Inputs may be any that keep to these rules, and one draw needn't show every extreme that they name: `kinds`: token 0 is an image patch and token 1 a text token.
All inputs are finite; a program needn't handle non-finite values.
Results may differ from the reference program's by a relative error of at most 0.0003.
Values may be sent and summed in bfloat16 or wider, within the bound.
No kernel may reach another device: no remote copies, remote signals or barrier semaphores. Data moves between devices by JAX's collectives and lax.ppermute only.
A program may use at most 128 MiB of HBM per device.

```python
import jax
import jax.numpy as jnp
from jax import lax

DIN_W = 4096
DOUT_W = 4096
BLK = 512
TOKENS = 49152
NBA = 8
NBG = 8


def token_scale(key):
    return jnp.exp(jax.random.uniform(key, (TOKENS,), jnp.float32, jnp.log(0.3), jnp.log(3.0)))


def token_cluster(key):
    return jax.random.randint(jax.random.fold_in(key, 5), (TOKENS,), 0, 64, dtype=jnp.int32)


def shape_rows(noise, table, cluster, scale, key, width):
    direction = table[cluster]
    mixed = noise + 0.6 * jnp.roll(noise, 1, axis=1) + 2.0 * direction
    column = jnp.exp(jax.random.uniform(key, (width,), jnp.float32, jnp.log(0.5), jnp.log(2.0)))
    rows = 0.25 * scale[:, None] * column[None, :] * mixed
    return jnp.clip(rows, -60.0, 60.0).astype(jnp.bfloat16)


def draw_acts(key, part):
    scale = token_scale(key)
    cluster = token_cluster(key)
    key = jax.random.fold_in(key, 11)
    first = jax.random.fold_in(key, 0)
    third = jax.random.fold_in(key, 2)
    fourth = jax.random.fold_in(key, 3)
    noise = jax.random.normal(first, (TOKENS, DIN_W), jnp.float32)
    table = jax.random.normal(fourth, (64, DIN_W), jnp.float32)
    return shape_rows(noise, table, cluster, scale, third, DIN_W)


def draw_grads(key, part):
    scale = token_scale(key)
    cluster = token_cluster(key)
    key = jax.random.fold_in(key, 13)
    first = jax.random.fold_in(key, 0)
    third = jax.random.fold_in(key, 2)
    fourth = jax.random.fold_in(key, 3)
    noise = jax.random.normal(first, (TOKENS, DOUT_W), jnp.float32)
    table = jax.random.normal(fourth, (64, DOUT_W), jnp.float32)
    return shape_rows(noise, table, cluster, scale, third, DOUT_W)


def draw_kinds(key, part):
    key = jax.random.fold_in(key, 7)
    first, second = jax.random.split(key)
    place = jnp.arange(TOKENS, dtype=jnp.int32)
    chance = jax.random.randint(first, (TOKENS,), 0, 1000, dtype=jnp.int32)
    limit = 300 + 600 * place // TOKENS
    kind_value = jax.random.randint(second, (TOKENS,), 1, 3, dtype=jnp.int32)
    kinds = jnp.where(chance < limit, kind_value, 0)
    kinds = jnp.where(place == 0, 1, kinds)
    kinds = jnp.where(place == 1, 2, kinds)
    return kinds.astype(jnp.int32)


def block_levels(own_key, dims, shards, low, largest):
    def one(position, blocks):
        draws = jax.random.uniform(jax.random.fold_in(jax.random.fold_in(own_key, 6), position), (blocks,), jnp.float32, low / len(shards), largest / len(shards))
        return jnp.repeat(jnp.exp(draws), dims[position] // blocks).reshape((-1,) + (1,) * (len(dims) - position - 1))

    factor_of = one(*shards[0])
    for cut in shards[1:]:
        factor_of = factor_of * one(*cut)
    return factor_of


def bell_draw(stream_key, dims, spread, most, cuts=(), held_as=jnp.bfloat16):
    result = spread * jax.random.normal(stream_key, dims, jnp.float32)
    if cuts:
        result = result * block_levels(stream_key, dims, cuts, -0.22, 0.18)
    return jnp.clip(result, -most, most).astype(held_as)


def setup_inputs(seed: int = 0) -> dict:
    keys = jax.random.split(jax.random.key(seed), 6)
    acts = draw_acts(jax.random.fold_in(keys[5], 71), 0)
    grads = draw_grads(jax.random.fold_in(keys[5], 71), 0)
    kinds = draw_kinds(jax.random.fold_in(keys[5], 71), 0)
    act_basis = bell_draw(keys[3], (NBA, BLK, BLK), BLK ** -0.5, 0.25, ((0, 4), (1, 64)))
    grad_basis = bell_draw(keys[4], (NBG, BLK, BLK), BLK ** -0.5, 0.25, ((0, 4), (1, 64)))
    return {"acts": acts, "grads": grads, "kinds": kinds, "act_basis": act_basis, "grad_basis": grad_basis}


def block_grams(weighted, plain, groups):
    def one_block(index):
        left = lax.dynamic_slice_in_dim(weighted, index * BLK, BLK, 1)
        right = lax.dynamic_slice_in_dim(plain, index * BLK, BLK, 1)
        return jnp.dot(left.T, right, preferred_element_type=jnp.float32)
    return lax.map(one_block, jnp.arange(groups, dtype=jnp.int32))


def block_project(plain, basis, groups):
    def one_block(index):
        right = lax.dynamic_slice_in_dim(plain, index * BLK, BLK, 1)
        return jnp.dot(right, basis[index], preferred_element_type=jnp.float32)
    stacked = lax.map(one_block, jnp.arange(groups, dtype=jnp.int32))
    return jnp.transpose(stacked, (1, 0, 2)).reshape(plain.shape[0], groups * BLK)


def reference(acts, grads, kinds, act_basis, grad_basis):
    image = (kinds == 1).astype(jnp.float32)
    text = (kinds == 2).astype(jnp.float32)
    n_image = jnp.sum(image)
    n_text = jnp.sum(text)
    weights = image / (2.0 * n_image) + text / (2.0 * n_text)
    weighted_acts = (weights[:, None] * acts).astype(jnp.bfloat16)
    weighted_grads = (weights[:, None] * grads).astype(jnp.bfloat16)
    act_factor = block_grams(weighted_acts, acts, NBA)
    grad_factor = block_grams(weighted_grads, grads, NBG)
    act_proj = block_project(acts, act_basis, NBA)
    grad_proj = block_project(grads, grad_basis, NBG)
    act_squares = (act_proj * act_proj).astype(jnp.bfloat16)
    grad_squares = (weights[:, None] * (grad_proj * grad_proj)).astype(jnp.bfloat16)
    eigenvalues = jnp.dot(grad_squares.T, act_squares, preferred_element_type=jnp.float32)
    return act_factor, grad_factor, eigenvalues
```

```python
import jax
import jax.numpy as jnp
from jax import lax
from jax.sharding import Mesh, PartitionSpec as P

HALF = jnp.float16
TOP = 14.0


def swap(value, axis, bits):
    size = lax.axis_size(axis)
    return lax.ppermute(value, axis, [(i, i ^ bits) for i in range(size)])


def shift(value, axis, step):
    size = lax.axis_size(axis)
    return lax.ppermute(value, axis, [(i, (i + step) % size) for i in range(size)])


def gather(value, axis):
    one, two, three = (shift(value, axis, step) for step in (1, 2, 3))
    twice = jnp.stack([three, two, one, value, three, two, one])
    return lax.dynamic_slice_in_dim(twice, 3 - lax.axis_index(axis), 4, 0)


def add_up(value, axis):
    return value + shift(value, axis, 1) + shift(value, axis, 2) + shift(value, axis, 3)


def pack(value):
    rows = value.reshape(-1, value.shape[-1])
    largest = jnp.max(jnp.abs(rows), axis=0, keepdims=True)
    power = jnp.ceil(jnp.log2(jnp.maximum(largest, 1e-30)))
    scaled = (rows * jnp.exp2(TOP - power)).astype(HALF)
    return jnp.concatenate([scaled, jnp.broadcast_to(power, (16, rows.shape[1])).astype(HALF)], 0)


def unpack(message, shape):
    power = message[-16:-15].astype(jnp.float32)
    return (message[:-16].astype(jnp.float32) * jnp.exp2(power - TOP)).reshape(shape)


def send(value, axis, bits):
    return unpack(swap(pack(value), axis, bits), value.shape)


def pick(value, dim, index):
    return lax.dynamic_index_in_dim(value, index, dim, keepdims=False)


def scatter_sum(value, dim, place, axis, first, second):
    part = lambda bits: pick(value, dim, place(bits))
    got = send(jnp.stack([part(first), part(first ^ second)]), axis, first)
    got_next = send(part(second) + got[1], axis, second)
    return part(0) + got[0] + got_next


def per_device(acts, grads, kinds, act_basis, grad_basis):
    tokens = acts.shape[0]
    groups, _, block = act_basis.shape
    x, zh, y = (lax.axis_index(a) for a in ("x", "zh", "y"))
    mp = lax.axis_index("zl") * 2 + lax.axis_index("core")

    grads_z = swap(grads, "zl", 1)
    grads_c = swap(grads, "core", 1)
    grads_zc = swap(grads_z, "core", 1)

    image = (kinds == 1).astype(jnp.float32)
    text = (kinds == 2).astype(jnp.float32)
    counts = jnp.concatenate(
        [jnp.full((4, 128), jnp.sum(image)), jnp.full((4, 128), jnp.sum(text))], 0
    )
    for axis in ("y", "x", "zh"):
        counts = add_up(counts, axis)
    weights = image / (2.0 * counts[0, 0]) + text / (2.0 * counts[4, 0])

    mine = jnp.concatenate([act_basis, grad_basis, swap(grad_basis, "zl", 1)], 0)
    mine = gather(mine, "zh")
    left = gather(gather(mine[:, :3], "x"), "y")
    right = gather(gather(mine[:, 3:], "y"), "x")
    left = jnp.transpose(left, (3, 1, 2, 0, 4, 5)).reshape(3, block, block)
    right = jnp.transpose(right, (3, 0, 2, 1, 4, 5)).reshape(3, block, block)
    act_blocks = left[:2]
    grad_blocks = jnp.concatenate([left[2:], right], 0)
    grad_blocks_c = swap(grad_blocks, "core", 1)

    def factor(values):
        weighted = (weights[:, None] * values).astype(jnp.bfloat16)
        return jnp.einsum(
            "tjr,tjc->jrc",
            weighted.reshape(tokens, groups, block),
            values.reshape(tokens, groups, block),
            preferred_element_type=jnp.float32,
        ).reshape(groups, 4, 4, 4, block // 64, block)

    act_sum = factor(acts)
    act_sum = scatter_sum(act_sum, 1, lambda b: x ^ b, "x", 1, 3)
    act_sum = scatter_sum(act_sum, 2, lambda b: y ^ b, "y", 1, 3)
    grad_sum = factor(grads)
    grad_sum = scatter_sum(grad_sum, 3, lambda b: y ^ b, "y", 3, 1)
    grad_sum = scatter_sum(grad_sum, 1, lambda b: x ^ b, "x", 3, 1)
    both = jnp.concatenate([act_sum, grad_sum], 0)
    part = lambda bits: pick(both, 1, zh ^ bits)
    both = part(0) + send(part(1), "zh", 1) + send(part(2), "zh", 2) + send(part(3), "zh", 3)

    def squares_of(values, blocks):
        rows = []
        for b in range(groups):
            projected = lax.dot_general(
                blocks[b],
                values[:, b * block : (b + 1) * block],
                (((0,), (1,)), ((), ())),
                preferred_element_type=jnp.float32,
            )
            rows.append((weights[None, :] * (projected * projected)).astype(jnp.bfloat16))
        return rows

    grad_squares = jnp.concatenate(
        squares_of(grads, grad_blocks[:2])
        + squares_of(grads_c, grad_blocks_c[:2])
        + squares_of(grads_z, grad_blocks[2:])
        + squares_of(grads_zc, grad_blocks_c[2:]),
        0,
    )
    columns = []
    for b in range(groups):
        projected = jnp.dot(
            acts[:, b * block : (b + 1) * block], act_blocks[b], preferred_element_type=jnp.float32
        )
        columns.append((projected * projected).astype(jnp.bfloat16))

    place_x = lambda b: x ^ b ^ mp
    place_y = lambda b: y ^ b
    streams = []
    for s in range(4):
        width = block // 2
        act_squares = columns[s // 2][:, (s % 2) * width : (s % 2 + 1) * width]
        total = jnp.dot(grad_squares, act_squares, preferred_element_type=jnp.float32)
        total = total.reshape(4, 4, 4, -1, width)
        first, second = ((1, 3), (3, 1))[s % 2]
        if s < 2:
            total = scatter_sum(total, 0, place_x, "x", first, second)
            total = scatter_sum(total, 1, place_y, "y", first, second)
        else:
            total = scatter_sum(total, 2, place_y, "y", first, second)
            total = scatter_sum(total, 0, place_x, "x", first, second)
        streams.append(total)
    total = jnp.concatenate(streams, 2)
    parts = lambda bits: pick(total, 0, zh ^ bits)
    eigenvalues = (
        parts(0) + send(parts(1), "zh", 1) + send(parts(2), "zh", 2) + send(parts(3), "zh", 3)
    )
    return both[:groups], both[groups:], eigenvalues


def solution(mesh):
    fine = Mesh(mesh.devices.reshape(4, 4, 4, 2, 2), ("x", "zh", "y", "zl", "core"))
    dp, mp = ("x", "zh", "y"), ("zl", "core")
    in_specs = (P(dp, mp), P(dp, mp), P(dp), P(mp, dp, None), P(mp, dp, None))
    out_specs = (P(mp, dp, None), P(mp, dp, None), P(dp, mp))
    return jax.shard_map(
        per_device, mesh=fine, in_specs=in_specs, out_specs=out_specs, check_vma=False
    )
```

```python
import jax
import jax.numpy as jnp
from jax import lax
from jax.experimental import pallas as pl
from jax.experimental.pallas import tpu as pltpu
from jax.sharding import Mesh, PartitionSpec as P

HALF = jnp.float16
TOP = 14.0


def swap(value, axis, bits):
    size = lax.axis_size(axis)
    return lax.ppermute(value, axis, [(i, i ^ bits) for i in range(size)])


def shift(value, axis, step):
    size = lax.axis_size(axis)
    return lax.ppermute(value, axis, [(i, (i + step) % size) for i in range(size)])


def add_up(value, axis):
    return value + shift(value, axis, 1) + shift(value, axis, 2) + shift(value, axis, 3)


def deal(value, axes):
    return lax.all_to_all(value, axes, 0, 0, tiled=True)


def gather(value, axes):
    count = lax.axis_size(axes)
    return deal(jnp.broadcast_to(value[None], (count,) + value.shape), axes)


def gather_ring(value, axis):
    one, two, three = (shift(value, axis, step) for step in (1, 2, 3))
    twice = jnp.stack([three, two, one, value, three, two, one])
    return lax.dynamic_slice_in_dim(twice, 3 - lax.axis_index(axis), 4, 0)


def pack(value):
    count, width = value.shape[0], value.shape[-1]
    rows = value.reshape(count, -1, width)
    largest = jnp.max(jnp.abs(rows), axis=(0, 1), keepdims=True)
    power = jnp.ceil(jnp.log2(jnp.maximum(largest, 1e-30)))
    scaled = (rows * jnp.exp2(TOP - power)).astype(HALF)
    extra = jnp.broadcast_to(power, (count, 16, width)).astype(HALF)
    return jnp.concatenate([scaled, extra], 1)


def unpack(got):
    scale = jnp.exp2(got[:, -16:-15].astype(jnp.float32) - TOP)
    return got[:, :-16].astype(jnp.float32) * scale


def send(value, axis, bits):
    return unpack(swap(pack(value[None])[0], axis, bits)[None]).reshape(value.shape)


def pick(value, dim, index):
    return lax.dynamic_index_in_dim(value, index, dim, keepdims=False)


def deal_sum(value, axes):
    return jnp.sum(unpack(deal(pack(value), axes)), axis=0).reshape(value.shape[1:])


def direct_sum(value, dim, axis):
    me = lax.axis_index(axis)
    part = lambda bits: pick(value, dim, me ^ bits)
    return part(0) + send(part(1), axis, 1) + send(part(2), axis, 2) + send(part(3), axis, 3)


def ring_sum(part, axis, first):
    second = 4 - first
    got = send(jnp.stack([part(first), part(2)]), axis, first)
    return part(0) + got[0] + send(part(second) + got[1], axis, second)


def after(value, *others):
    return lax.optimization_barrier((value, *others))[0]


def split(total):
    high = jnp.floor(total * (1 / 256))
    return jnp.concatenate([high, total - 256 * high], 1).astype(jnp.bfloat16)


def join(halves):
    wide = halves.astype(jnp.float32)
    middle = wide.shape[-1] // 2
    return 256 * wide[..., :middle] + wide[..., middle:]


def squared(basis, values, weights):
    projected = lax.dot_general(
        basis, values, (((0,), (1,)), ((), ())), preferred_element_type=jnp.float32
    )
    return (weights * (projected * projected)).astype(jnp.bfloat16)


def store(ref, lead, half, y, rows):
    for position in range(8):
        high, low = position // 4, position % 4
        ref[lead, low ^ y, 2 * half + high] = rows[position * 64 : (position + 1) * 64]


def own_kernel(
    place, weights, grads, grads_z, basis, acts, act_basis, squares, act_squares, held, blocks, sems
):
    copies = [
        pltpu.make_async_copy(grads, held.at[0], sems.at[0]),
        pltpu.make_async_copy(basis, blocks.at[pl.ds(0, 4)], sems.at[1]),
        pltpu.make_async_copy(grads_z, held.at[1], sems.at[2]),
        pltpu.make_async_copy(act_basis, blocks.at[pl.ds(4, 2)], sems.at[3]),
        pltpu.make_async_copy(acts, held.at[2], sems.at[4]),
    ]
    for copy in copies:
        copy.start()
    width = basis.shape[-1]
    copies[0].wait()
    copies[1].wait()
    for j in range(2):
        if j == 1:
            copies[2].wait()
        for b in range(2):
            values = held[j, :, b * width : (b + 1) * width]
            store(squares, j, b, place[1], squared(blocks[2 * j + b], values, weights[...]))
    copies[3].wait()
    copies[4].wait()
    for b in range(2):
        projected = jnp.dot(
            held[2, :, b * width : (b + 1) * width],
            blocks[4 + b],
            preferred_element_type=jnp.float32,
        )
        act_squares[:, b * width : (b + 1) * width] = (projected * projected).astype(jnp.bfloat16)


def product(squares, act_squares, lead, s, out):
    width = out.shape[-1]
    columns = act_squares[:, s * width : (s + 1) * width]
    tokens = columns.shape[0]

    def one(i, carry):
        if s < 2:
            rows = squares[lead + i]
        else:
            rows = squares[i, lead : lead + out.shape[1] // 256]
        out[i] = jnp.dot(
            rows.reshape(-1, tokens), columns, preferred_element_type=jnp.float32
        )
        return carry

    lax.fori_loop(0, out.shape[0], one, 0)


def send_kernel(
    place, weights, own, act, grads_c, grads_zc, basis, m0, m1, m2, m3, out,
    squares, act_squares, held, blocks, sum_x, sum_y, sems,
):
    copies = [
        pltpu.make_async_copy(grads_c, held.at[0], sems.at[0]),
        pltpu.make_async_copy(basis, blocks, sems.at[1]),
        pltpu.make_async_copy(grads_zc, held.at[1], sems.at[2]),
        pltpu.make_async_copy(own.at[0], squares.at[place[0]], sems.at[3]),
        pltpu.make_async_copy(own.at[1], squares.at[place[0] ^ 2], sems.at[4]),
        pltpu.make_async_copy(act, act_squares, sems.at[5]),
    ]
    for copy in copies:
        copy.start()
    width = basis.shape[-1]
    copies[0].wait()
    copies[1].wait()
    for j in range(2):
        if j == 1:
            copies[2].wait()
        for b in range(2):
            values = held[j, :, b * width : (b + 1) * width]
            rows = squared(blocks[2 * j + b], values, weights[...])
            store(squares, place[0] ^ (2 * j + 1), b, place[1], rows)
    for copy in copies[3:]:
        copy.wait()
    results = [pltpu.make_async_copy(squares, out, sems.at[0])]
    results[0].start()
    for s, (target, part) in enumerate(
        ((m0, sum_x.at[0]), (m1, sum_x.at[1]), (m2, sum_y.at[0]), (m3, sum_y.at[1]))
    ):
        product(squares, act_squares, 1 + s % 2, s, part)
        results.append(pltpu.make_async_copy(part, target, sems.at[1 + s]))
        results[-1].start()
    for copy in results:
        copy.wait()


def keep_kernel(squares_in, act_in, *refs):
    outs, (squares, act_squares, parts, sems) = refs[:8], refs[8:]
    first = pltpu.make_async_copy(squares_in, squares, sems.at[8])
    second = pltpu.make_async_copy(act_in, act_squares, sems.at[9])
    first.start()
    second.start()
    first.wait()
    second.wait()
    results = []
    for s in range(4):
        for k, lead in enumerate((0, (3, 1)[s % 2])):
            part = parts.at[2 * s + k]
            product(squares, act_squares, lead, s, part if s >= 2 else part.reshape(1, 1024, 256))
            results.append(pltpu.make_async_copy(part, outs[2 * s + k], sems.at[2 * s + k]))
            results[-1].start()
    for copy in results:
        copy.wait()


ANY = pl.BlockSpec(memory_space=pl.ANY)
SMEM = pl.BlockSpec(memory_space=pltpu.SMEM)
VMEM = pl.BlockSpec(memory_space=pltpu.VMEM)


def call(kernel, outs, ins, out_specs, scratch, flops, bytes_accessed, *args):
    return pl.pallas_call(
        kernel,
        out_shape=outs,
        in_specs=ins,
        out_specs=out_specs,
        scratch_shapes=scratch,
        compiler_params=pltpu.CompilerParams(vmem_limit_bytes=44 * 2**20),
        cost_estimate=pl.CostEstimate(
            flops=flops, bytes_accessed=bytes_accessed, transcendentals=0
        ),
    )(*args)


def per_device(acts, grads, kinds, act_basis, grad_basis):
    tokens = acts.shape[0]
    groups, piece, block = act_basis.shape
    x, y, zl = (lax.axis_index(a) for a in ("x", "y", "zl"))
    mp = zl * 2 + lax.axis_index("core")

    image = (kinds == 1).astype(jnp.float32)
    text = (kinds == 2).astype(jnp.float32)
    counts = jnp.concatenate(
        [jnp.full((piece, block // 4), jnp.sum(kind)) for kind in (image, text)], 1
    )
    line = gather(jnp.concatenate([act_basis, grad_basis, split(counts)[None]], 0), ("zh", "zl"))
    line = line.reshape(4, 2, 2 * groups + 1, piece, block)
    own = pick(line, 1, zl)
    other = pick(line, 1, 1 - zl)[:, groups:-1]

    grads_z = swap(after(grads, line), "zl", 1)
    grads_zc = swap(grads_z, "core", 1)

    counts = jnp.sum(join(own[:, -1]), axis=0)
    left = own[:, :3].reshape(12, piece, block)
    left = gather(jnp.concatenate([left, split(counts)[None]], 0), "x")
    counts = add_up(jnp.sum(join(left[:, -1]), axis=0), "y")
    grads_c = swap(after(grads, counts), "core", 1)
    left = gather(left[:, :-1], "y").reshape(4, 4, 4, 3, piece, block)
    right = gather_ring(gather_ring(jnp.concatenate([own[:, 3:-1], other], 1), "y"), "x")
    left = jnp.transpose(left, (3, 1, 2, 0, 4, 5)).reshape(3, block, block)
    right = jnp.transpose(right, (3, 0, 2, 1, 4, 5)).reshape(3, block, block)
    grad_blocks = jnp.concatenate([left[2:], right], 0)
    grad_blocks_c = swap(grad_blocks, "core", 1)
    weights = image / (2.0 * counts[0, 0]) + text / (2.0 * counts[0, block // 4])

    def factor(values):
        weighted = (weights[:, None] * values).astype(jnp.bfloat16)
        return jnp.einsum(
            "tjr,tjc->jrc",
            weighted.reshape(tokens, groups, block),
            values.reshape(tokens, groups, block),
            preferred_element_type=jnp.float32,
        ).reshape(groups, 4, 4, 4, piece, block)

    factors = jnp.concatenate([factor(acts), factor(grads)], 0)
    factors = pack(jnp.transpose(factors, (2, 1, 3, 0, 4, 5)))
    factors = deal(after(factors, grads_z), "zh")

    f32, bf16 = jnp.float32, jnp.bfloat16
    like = jax.ShapeDtypeStruct
    row = weights[None, :]
    place = jnp.stack([mp ^ x, y]).astype(jnp.int32)
    wide = groups * block
    own_squares, act_squares = call(
        own_kernel,
        [like((2, 4, 4, 64, tokens), bf16), like((tokens, wide), bf16)],
        [SMEM, VMEM, ANY, ANY, ANY, ANY, ANY],
        [VMEM, VMEM],
        [
            pltpu.VMEM((3, tokens, wide), bf16),
            pltpu.VMEM((6, block, block), bf16),
            pltpu.SemaphoreType.DMA((5,)),
        ],
        12 * tokens * block * block,
        14 * 2**20,
        place, row, grads, grads_z, grad_blocks, acts, left[:2],
    )
    messages = call(
        send_kernel,
        [like((2, 1024, 256), f32)] * 2
        + [like((4, 512, 256), f32)] * 2
        + [like((4, 4, 4, 64, tokens), bf16)],
        [SMEM, VMEM, ANY, ANY, ANY, ANY, ANY],
        [ANY] * 5,
        [
            pltpu.VMEM((4, 4, 4, 64, tokens), bf16),
            pltpu.VMEM((tokens, wide), bf16),
            pltpu.VMEM((2, tokens, wide), bf16),
            pltpu.VMEM((4, block, block), bf16),
            pltpu.VMEM((2, 2, 1024, 256), f32),
            pltpu.VMEM((2, 4, 512, 256), f32),
            pltpu.SemaphoreType.DMA((6,)),
        ],
        8 * tokens * block * block + 4 * tokens * wide * wide,
        24 * 2**20,
        place, row, own_squares, act_squares, grads_c, grads_zc, grad_blocks_c,
    )
    packed = [pack(m.reshape(1, -1, 256))[0] for m in messages[:4]]
    squares = after(messages[4], *packed)
    kept = call(
        keep_kernel,
        [like((4, 256, 256), f32)] * 8,
        [ANY, ANY],
        [ANY] * 8,
        [
            pltpu.VMEM((4, 4, 4, 64, tokens), bf16),
            pltpu.VMEM((tokens, wide), bf16),
            pltpu.VMEM((8, 4, 256, 256), f32),
            pltpu.SemaphoreType.DMA((10,)),
        ],
        4 * tokens * wide * wide,
        16 * 2**20,
        squares, act_squares,
    )

    streams = []
    for s in range(4):
        axis, other = (("x", "y"), ("y", "x"))[s // 2]
        first = (1, 3)[s % 2]
        got = unpack(swap(packed[s], axis, first)[None])
        got = got.reshape((2, 4, 256, 256) if s < 2 else (4, 2, 256, 256))
        near, far = (lax.index_in_dim(got, k ^ (s % 2), s // 2, False) for k in range(2))
        total = kept[2 * s] + near + send(kept[2 * s + 1] + far, axis, 4 - first)
        if s == 0:
            halfway = total
        streams.append(ring_sum(lambda bits: total[bits], other, first).reshape(4, 64, 256))
    eigenvalues = direct_sum(jnp.concatenate(streams, 2), 0, "zh")

    factors = jnp.sum(unpack(after(factors, halfway)), axis=0)
    factors = deal_sum(factors.reshape(16, 2 * groups, piece, block), ("x", "y"))
    return factors[:groups], factors[groups:], eigenvalues


def solution(mesh):
    fine = Mesh(mesh.devices.reshape(4, 4, 4, 2, 2), ("x", "zh", "y", "zl", "core"))
    dp, mp = ("x", "zh", "y"), ("zl", "core")
    in_specs = (P(dp, mp), P(dp, mp), P(dp), P(mp, dp, None), P(mp, dp, None))
    out_specs = (P(mp, dp, None), P(mp, dp, None), P(dp, mp))
    return jax.shard_map(
        per_device, mesh=fine, in_specs=in_specs, out_specs=out_specs, check_vma=False
    )
```

```python
import jax
import jax.numpy as jnp
from jax import lax
from jax.experimental import pallas as pl
from jax.experimental.pallas import tpu as pltpu
from jax.sharding import Mesh, PartitionSpec as P

HALF = jnp.float16
TOP = 14.0


def swap(value, axis, bits):
    size = lax.axis_size(axis)
    return lax.ppermute(value, axis, [(i, i ^ bits) for i in range(size)])


def shift(value, axis, step):
    size = lax.axis_size(axis)
    return lax.ppermute(value, axis, [(i, (i + step) % size) for i in range(size)])


def add_up(value, axis):
    return value + shift(value, axis, 1) + shift(value, axis, 2) + shift(value, axis, 3)


def deal(value, axes):
    return lax.all_to_all(value, axes, 0, 0, tiled=True)


def gather(value, axes):
    count = lax.axis_size(axes)
    return deal(jnp.broadcast_to(value[None], (count,) + value.shape), axes)


def gather_ring(value, axis):
    one, two, three = (shift(value, axis, step) for step in (1, 2, 3))
    twice = jnp.stack([three, two, one, value, three, two, one])
    return lax.dynamic_slice_in_dim(twice, 3 - lax.axis_index(axis), 4, 0)


def pack(value):
    count, width = value.shape[0], value.shape[-1]
    rows = value.reshape(count, -1, width)
    largest = jnp.max(jnp.abs(rows), axis=(0, 1), keepdims=True)
    power = jnp.ceil(jnp.log2(jnp.maximum(largest, 1e-30)))
    scaled = (rows * jnp.exp2(TOP - power)).astype(HALF)
    extra = jnp.broadcast_to(power, (count, 16, width)).astype(HALF)
    return jnp.concatenate([scaled, extra], 1)


def unpack(got):
    scale = jnp.exp2(got[:, -16:-15].astype(jnp.float32) - TOP)
    return got[:, :-16].astype(jnp.float32) * scale


def send(value, axis, bits):
    return unpack(swap(pack(value[None])[0], axis, bits)[None]).reshape(value.shape)


def pick(value, dim, index):
    return lax.dynamic_index_in_dim(value, index, dim, keepdims=False)


def deal_sum(value, axes):
    return jnp.sum(unpack(deal(pack(value), axes)), axis=0).reshape(value.shape[1:])


def direct_sum(value, dim, axis):
    me = lax.axis_index(axis)
    part = lambda bits: pick(value, dim, me ^ bits)
    return part(0) + send(part(1), axis, 1) + send(part(2), axis, 2) + send(part(3), axis, 3)


def ring_sum(part, axis, first):
    second = 4 - first
    got = send(jnp.stack([part(first), part(2)]), axis, first)
    return part(0) + got[0] + send(part(second) + got[1], axis, second)


def after(value, *others):
    return lax.optimization_barrier((value, *others))[0]


def split(total):
    high = jnp.floor(total * (1 / 256))
    return jnp.concatenate([high, total - 256 * high], 1).astype(jnp.bfloat16)


def join(halves):
    wide = halves.astype(jnp.float32)
    middle = wide.shape[-1] // 2
    return 256 * wide[..., :middle] + wide[..., middle:]


def squared(basis, values, weights):
    projected = lax.dot_general(
        basis, values, (((0,), (1,)), ((), ())), preferred_element_type=jnp.float32
    )
    return (weights * (projected * projected)).astype(jnp.bfloat16)


def store(ref, lead, half, y, rows):
    for position in range(8):
        high, low = position // 4, position % 4
        ref[lead, low ^ y, 2 * half + high] = rows[position * 64 : (position + 1) * 64]


def factor_kernel(weights, acts, grads, out, held, sems):
    copies = [pltpu.make_async_copy(v, held.at[i], sems.at[i]) for i, v in enumerate((acts, grads))]
    for copy in copies:
        copy.start()
    width = out.shape[-1]
    for i in range(2):
        copies[i].wait()
        for b in range(2):
            values = held[i, :, b * width : (b + 1) * width]
            weighted = (weights[...] * values).astype(jnp.bfloat16)
            gram = lax.dot_general(
                weighted, values, (((0,), (0,)), ((), ())), preferred_element_type=jnp.float32
            )
            for p in range(16):
                rows = gram[p * 32 : (p + 1) * 32].reshape(4, 8, width)
                out[p % 4, p // 4, :, 2 * i + b] = rows


def own_kernel(
    place, weights, grads, grads_z, basis, acts, act_basis, squares, act_squares, held, blocks, sems
):
    copies = [
        pltpu.make_async_copy(grads, held.at[0], sems.at[0]),
        pltpu.make_async_copy(basis, blocks.at[pl.ds(0, 4)], sems.at[1]),
        pltpu.make_async_copy(grads_z, held.at[1], sems.at[2]),
        pltpu.make_async_copy(act_basis, blocks.at[pl.ds(4, 2)], sems.at[3]),
        pltpu.make_async_copy(acts, held.at[2], sems.at[4]),
    ]
    for copy in copies:
        copy.start()
    width = basis.shape[-1]
    copies[0].wait()
    copies[1].wait()
    for j in range(2):
        if j == 1:
            copies[2].wait()
        for b in range(2):
            values = held[j, :, b * width : (b + 1) * width]
            store(squares, j, b, place[1], squared(blocks[2 * j + b], values, weights[...]))
    copies[3].wait()
    copies[4].wait()
    for b in range(2):
        projected = jnp.dot(
            held[2, :, b * width : (b + 1) * width],
            blocks[4 + b],
            preferred_element_type=jnp.float32,
        )
        act_squares[:, b * width : (b + 1) * width] = (projected * projected).astype(jnp.bfloat16)


def product(squares, act_squares, lead, s, out):
    width = out.shape[-1]
    columns = act_squares[:, s * width : (s + 1) * width]
    tokens = columns.shape[0]

    def one(i, carry):
        if s < 2:
            rows = squares[lead + i]
        else:
            rows = squares[i, lead : lead + out.shape[1] // 256]
        out[i] = jnp.dot(
            rows.reshape(-1, tokens), columns, preferred_element_type=jnp.float32
        )
        return carry

    lax.fori_loop(0, out.shape[0], one, 0)


def send_kernel(
    place, weights, own, act, grads_c, grads_zc, basis, m0, m1, m2, m3, out,
    squares, act_squares, held, blocks, sems,
):
    copies = [
        pltpu.make_async_copy(grads_c, held.at[0], sems.at[0]),
        pltpu.make_async_copy(basis, blocks, sems.at[1]),
        pltpu.make_async_copy(grads_zc, held.at[1], sems.at[2]),
        pltpu.make_async_copy(own.at[0], squares.at[place[0]], sems.at[3]),
        pltpu.make_async_copy(own.at[1], squares.at[place[0] ^ 2], sems.at[4]),
        pltpu.make_async_copy(act, act_squares, sems.at[5]),
    ]
    for copy in copies:
        copy.start()
    width = basis.shape[-1]
    copies[0].wait()
    copies[1].wait()
    for j in range(2):
        if j == 1:
            copies[2].wait()
        for b in range(2):
            values = held[j, :, b * width : (b + 1) * width]
            rows = squared(blocks[2 * j + b], values, weights[...])
            store(squares, place[0] ^ (2 * j + 1), b, place[1], rows)
    for copy in copies[3:]:
        copy.wait()
    results = [pltpu.make_async_copy(squares, out, sems.at[0])]
    results[0].start()
    for s, part in enumerate((m0, m1, m2, m3)):
        product(squares, act_squares, 1 + s % 2, s, part)
    for copy in results:
        copy.wait()


def keep_kernel(squares_in, act_in, *refs):
    outs, (squares, act_squares, sems) = refs[:8], refs[8:]
    first = pltpu.make_async_copy(squares_in, squares, sems.at[0])
    second = pltpu.make_async_copy(act_in, act_squares, sems.at[1])
    first.start()
    second.start()
    first.wait()
    second.wait()
    for s in range(4):
        for k, lead in enumerate((0, (3, 1)[s % 2])):
            part = outs[2 * s + k]
            product(squares, act_squares, lead, s, part if s >= 2 else part.reshape(1, 1024, 256))


ANY = pl.BlockSpec(memory_space=pl.ANY)
SMEM = pl.BlockSpec(memory_space=pltpu.SMEM)
VMEM = pl.BlockSpec(memory_space=pltpu.VMEM)


def call(kernel, outs, ins, out_specs, scratch, flops, bytes_accessed, *args):
    return pl.pallas_call(
        kernel,
        out_shape=outs,
        in_specs=ins,
        out_specs=out_specs,
        scratch_shapes=scratch,
        compiler_params=pltpu.CompilerParams(vmem_limit_bytes=44 * 2**20),
        cost_estimate=pl.CostEstimate(
            flops=flops, bytes_accessed=bytes_accessed, transcendentals=0
        ),
    )(*args)


def per_device(acts, grads, kinds, act_basis, grad_basis):
    tokens = acts.shape[0]
    groups, piece, block = act_basis.shape
    wide = groups * block
    f32, bf16 = jnp.float32, jnp.bfloat16
    like = jax.ShapeDtypeStruct
    x, y, zl = (lax.axis_index(a) for a in ("x", "y", "zl"))
    mp = zl * 2 + lax.axis_index("core")

    image = (kinds == 1).astype(jnp.float32)
    text = (kinds == 2).astype(jnp.float32)
    counts = jnp.concatenate(
        [jnp.full((piece, block // 4), jnp.sum(kind)) for kind in (image, text)], 1
    )
    own = gather_ring(jnp.concatenate([act_basis, grad_basis, split(counts)[None]], 0), "zh")
    other = swap(own[:, groups:-1], "zl", 1)

    grads_z = swap(after(grads, other), "zl", 1)
    grads_zc = swap(grads_z, "core", 1)

    counts = jnp.sum(join(own[:, -1]), axis=0)
    left = own[:, :3].reshape(12, piece, block)
    left = gather(jnp.concatenate([left, split(counts)[None]], 0), "x")
    counts = add_up(jnp.sum(join(left[:, -1]), axis=0), "y")
    grads_c = swap(after(grads, counts), "core", 1)
    left = gather(left[:, :-1], "y").reshape(4, 4, 4, 3, piece, block)
    right = gather_ring(gather_ring(jnp.concatenate([own[:, 3:-1], other], 1), "y"), "x")
    weights = image / (2.0 * counts[0, 0]) + text / (2.0 * counts[0, block // 4])

    factors = call(
        factor_kernel,
        like((4, 4, 4, 2 * groups, piece, block), f32),
        [VMEM, ANY, ANY],
        VMEM,
        [
            pltpu.VMEM((2, tokens, wide), bf16),
            pltpu.SemaphoreType.DMA((2,)),
        ],
        8 * tokens * block * block,
        8 * 2**20,
        weights[:, None], acts, grads,
    )
    factors = pack(factors)
    left, right = after(left, factors), after(right, factors)
    factors = deal(after(factors, grads_z), "zh")

    left = jnp.transpose(left, (3, 1, 2, 0, 4, 5)).reshape(3, block, block)
    right = jnp.transpose(right, (3, 0, 2, 1, 4, 5)).reshape(3, block, block)
    grad_blocks = jnp.concatenate([left[2:], right], 0)
    grad_blocks_c = swap(grad_blocks, "core", 1)

    row = weights[None, :]
    place = jnp.stack([mp ^ x, y]).astype(jnp.int32)
    own_squares, act_squares = call(
        own_kernel,
        [like((2, 4, 4, 64, tokens), bf16), like((tokens, wide), bf16)],
        [SMEM, VMEM, ANY, ANY, ANY, ANY, ANY],
        [VMEM, VMEM],
        [
            pltpu.VMEM((3, tokens, wide), bf16),
            pltpu.VMEM((6, block, block), bf16),
            pltpu.SemaphoreType.DMA((5,)),
        ],
        12 * tokens * block * block,
        14 * 2**20,
        place, row, grads, grads_z, grad_blocks, acts, left[:2],
    )
    messages = call(
        send_kernel,
        [like((2, 1024, 256), f32)] * 2
        + [like((4, 512, 256), f32)] * 2
        + [like((4, 4, 4, 64, tokens), bf16)],
        [SMEM, VMEM, ANY, ANY, ANY, ANY, ANY],
        [VMEM] * 4 + [ANY],
        [
            pltpu.VMEM((4, 4, 4, 64, tokens), bf16),
            pltpu.VMEM((tokens, wide), bf16),
            pltpu.VMEM((2, tokens, wide), bf16),
            pltpu.VMEM((4, block, block), bf16),
            pltpu.SemaphoreType.DMA((6,)),
        ],
        8 * tokens * block * block + 4 * tokens * wide * wide,
        24 * 2**20,
        place, row, own_squares, act_squares, grads_c, grads_zc, grad_blocks_c,
    )
    packed = [pack(m.reshape(1, -1, 256))[0] for m in messages[:4]]
    squares = after(messages[4], *packed)
    kept = call(
        keep_kernel,
        [like((4, 256, 256), f32)] * 8,
        [ANY, ANY],
        [VMEM] * 8,
        [
            pltpu.VMEM((4, 4, 4, 64, tokens), bf16),
            pltpu.VMEM((tokens, wide), bf16),
            pltpu.SemaphoreType.DMA((2,)),
        ],
        4 * tokens * wide * wide,
        16 * 2**20,
        squares, act_squares,
    )

    streams = []
    for s in range(4):
        axis, other = (("x", "y"), ("y", "x"))[s // 2]
        first = (1, 3)[s % 2]
        got = unpack(swap(packed[s], axis, first)[None])
        got = got.reshape((2, 4, 256, 256) if s < 2 else (4, 2, 256, 256))
        near, far = (lax.index_in_dim(got, k ^ (s % 2), s // 2, False) for k in range(2))
        total = kept[2 * s] + near + send(kept[2 * s + 1] + far, axis, 4 - first)
        streams.append(ring_sum(lambda bits: total[bits], other, first).reshape(4, 64, 256))
    eigenvalues = direct_sum(jnp.concatenate(streams, 2), 0, "zh")

    factors = jnp.sum(unpack(after(factors, *streams)), axis=0)
    factors = deal_sum(factors.reshape(16, 2 * groups, piece, block), ("x", "y"))
    return factors[:groups], factors[groups:], eigenvalues


def solution(mesh):
    fine = Mesh(mesh.devices.reshape(4, 4, 4, 2, 2), ("x", "zh", "y", "zl", "core"))
    dp, mp = ("x", "zh", "y"), ("zl", "core")
    in_specs = (P(dp, mp), P(dp, mp), P(dp), P(mp, dp, None), P(mp, dp, None))
    out_specs = (P(mp, dp, None), P(mp, dp, None), P(dp, mp))
    return jax.shard_map(
        per_device, mesh=fine, in_specs=in_specs, out_specs=out_specs, check_vma=False
    )
```

```python
import jax
import jax.numpy as jnp
from jax import lax
from jax.experimental import pallas as pl
from jax.experimental.pallas import tpu as pltpu
from jax.sharding import Mesh, PartitionSpec as P

HALF = jnp.float16
TOP = 14.0


def swap(value, axis, bits):
    size = lax.axis_size(axis)
    return lax.ppermute(value, axis, [(i, i ^ bits) for i in range(size)])


def shift(value, axis, step):
    size = lax.axis_size(axis)
    return lax.ppermute(value, axis, [(i, (i + step) % size) for i in range(size)])


def add_up(value, axis):
    return value + shift(value, axis, 1) + shift(value, axis, 2) + shift(value, axis, 3)


def deal(value, axes):
    return lax.all_to_all(value, axes, 0, 0, tiled=True)


def gather(value, axes):
    count = lax.axis_size(axes)
    return deal(jnp.broadcast_to(value[None], (count,) + value.shape), axes)


def gather_ring(value, axis):
    one, two, three = (shift(value, axis, step) for step in (1, 2, 3))
    twice = jnp.stack([three, two, one, value, three, two, one])
    return lax.dynamic_slice_in_dim(twice, 3 - lax.axis_index(axis), 4, 0)


def pack(value):
    count, width = value.shape[0], value.shape[-1]
    rows = value.reshape(count, -1, width)
    largest = jnp.max(jnp.abs(rows), axis=(0, 1), keepdims=True)
    power = jnp.ceil(jnp.log2(jnp.maximum(largest, 1e-30)))
    scaled = (rows * jnp.exp2(TOP - power)).astype(HALF)
    extra = jnp.broadcast_to(power, (count, 16, width)).astype(HALF)
    return jnp.concatenate([scaled, extra], 1)


def scale_of(message):
    return jnp.exp2(message[-16:-15].astype(jnp.float32) - TOP)


def unpack(got):
    scale = jnp.exp2(got[:, -16:-15].astype(jnp.float32) - TOP)
    return got[:, :-16].astype(jnp.float32) * scale


def send(value, axis, bits):
    return unpack(swap(pack(value[None])[0], axis, bits)[None]).reshape(value.shape)


def pick(value, dim, index):
    return lax.dynamic_index_in_dim(value, index, dim, keepdims=False)


def direct_sum(value, dim, axis):
    me = lax.axis_index(axis)
    part = lambda bits: pick(value, dim, me ^ bits)
    return part(0) + send(part(1), axis, 1) + send(part(2), axis, 2) + send(part(3), axis, 3)


def after(value, *others):
    return lax.optimization_barrier((value, *others))[0]


def split(total):
    high = jnp.floor(total * (1 / 256))
    return jnp.concatenate([high, total - 256 * high], 1).astype(jnp.bfloat16)


def join(halves):
    wide = halves.astype(jnp.float32)
    middle = wide.shape[-1] // 2
    return 256 * wide[..., :middle] + wide[..., middle:]


def squared(basis, values, weights):
    projected = lax.dot_general(
        basis, values, (((0,), (1,)), ((), ())), preferred_element_type=jnp.float32
    )
    return (weights * (projected * projected)).astype(jnp.bfloat16)


def store(ref, lead, half, y, rows):
    for position in range(8):
        high, low = position // 4, position % 4
        ref[lead, low ^ y, 2 * half + high] = rows[position * 64 : (position + 1) * 64]


def factor_kernel(weights, acts, grads, out, held, sems):
    copies = [pltpu.make_async_copy(v, held.at[i], sems.at[i]) for i, v in enumerate((acts, grads))]
    for copy in copies:
        copy.start()
    width = out.shape[-1]
    for i in range(2):
        copies[i].wait()
        for b in range(2):
            values = held[i, :, b * width : (b + 1) * width]
            weighted = (weights[...] * values).astype(jnp.bfloat16)
            gram = lax.dot_general(
                weighted, values, (((0,), (0,)), ((), ())), preferred_element_type=jnp.float32
            )
            for p in range(16):
                rows = gram[p * 32 : (p + 1) * 32].reshape(4, 8, width)
                out[p % 4, p // 4, :, 2 * i + b] = rows


def own_kernel(
    place, weights, grads, grads_z, basis, acts, act_basis, squares, act_squares, held, blocks, sems
):
    copies = [
        pltpu.make_async_copy(grads, held.at[0], sems.at[0]),
        pltpu.make_async_copy(basis, blocks.at[pl.ds(0, 4)], sems.at[1]),
        pltpu.make_async_copy(grads_z, held.at[1], sems.at[2]),
        pltpu.make_async_copy(act_basis, blocks.at[pl.ds(4, 2)], sems.at[3]),
        pltpu.make_async_copy(acts, held.at[2], sems.at[4]),
    ]
    for copy in copies:
        copy.start()
    width = basis.shape[-1]
    copies[0].wait()
    copies[1].wait()
    for j in range(2):
        if j == 1:
            copies[2].wait()
        for b in range(2):
            values = held[j, :, b * width : (b + 1) * width]
            store(squares, j, b, place[1], squared(blocks[2 * j + b], values, weights[...]))
    copies[3].wait()
    copies[4].wait()
    for b in range(2):
        projected = jnp.dot(
            held[2, :, b * width : (b + 1) * width],
            blocks[4 + b],
            preferred_element_type=jnp.float32,
        )
        act_squares[:, b * width : (b + 1) * width] = (projected * projected).astype(jnp.bfloat16)


def product(squares, act_squares, lead, s, out):
    width = out.shape[-1]
    columns = act_squares[:, s * width : (s + 1) * width]
    tokens = columns.shape[0]

    def one(i, carry):
        if s < 2:
            rows = squares[lead + i]
        else:
            rows = squares[i, lead : lead + out.shape[1] // 256]
        out[i] = jnp.dot(
            rows.reshape(-1, tokens), columns, preferred_element_type=jnp.float32
        )
        return carry

    lax.fori_loop(0, out.shape[0], one, 0)


def send_kernel(
    place, weights, own, act, grads_c, grads_zc, basis, m0, m1, m2, m3, out,
    squares, act_squares, held, blocks, sems,
):
    copies = [
        pltpu.make_async_copy(grads_c, held.at[0], sems.at[0]),
        pltpu.make_async_copy(basis, blocks, sems.at[1]),
        pltpu.make_async_copy(grads_zc, held.at[1], sems.at[2]),
        pltpu.make_async_copy(own.at[0], squares.at[place[0]], sems.at[3]),
        pltpu.make_async_copy(own.at[1], squares.at[place[0] ^ 2], sems.at[4]),
        pltpu.make_async_copy(act, act_squares, sems.at[5]),
    ]
    for copy in copies:
        copy.start()
    width = basis.shape[-1]
    copies[0].wait()
    copies[1].wait()
    for j in range(2):
        if j == 1:
            copies[2].wait()
        for b in range(2):
            values = held[j, :, b * width : (b + 1) * width]
            rows = squared(blocks[2 * j + b], values, weights[...])
            store(squares, place[0] ^ (2 * j + 1), b, place[1], rows)
    for copy in copies[3:]:
        copy.wait()
    results = [pltpu.make_async_copy(squares, out, sems.at[0])]
    results[0].start()
    for s, part in enumerate((m0, m1, m2, m3)):
        product(squares, act_squares, 1 + s % 2, s, part)
    for copy in results:
        copy.wait()


def keep_kernel(squares_in, act_in, *refs):
    outs, (squares, act_squares, sems) = refs[:8], refs[8:]
    first = pltpu.make_async_copy(squares_in, squares, sems.at[0])
    second = pltpu.make_async_copy(act_in, act_squares, sems.at[1])
    first.start()
    second.start()
    first.wait()
    second.wait()
    for s in range(4):
        for k, lead in enumerate((0, (3, 1)[s % 2])):
            part = outs[2 * s + k]
            product(squares, act_squares, lead, s, part if s >= 2 else part.reshape(1, 1024, 256))


ANY = pl.BlockSpec(memory_space=pl.ANY)
SMEM = pl.BlockSpec(memory_space=pltpu.SMEM)
VMEM = pl.BlockSpec(memory_space=pltpu.VMEM)


def call(kernel, outs, ins, out_specs, scratch, flops, bytes_accessed, *args):
    return pl.pallas_call(
        kernel,
        out_shape=outs,
        in_specs=ins,
        out_specs=out_specs,
        scratch_shapes=scratch,
        compiler_params=pltpu.CompilerParams(vmem_limit_bytes=44 * 2**20),
        cost_estimate=pl.CostEstimate(
            flops=flops, bytes_accessed=bytes_accessed, transcendentals=0
        ),
    )(*args)


def per_device(acts, grads, kinds, act_basis, grad_basis):
    tokens = acts.shape[0]
    groups, piece, block = act_basis.shape
    wide = groups * block
    f32, bf16 = jnp.float32, jnp.bfloat16
    like = jax.ShapeDtypeStruct
    x, y, zl = (lax.axis_index(a) for a in ("x", "y", "zl"))
    mp = zl * 2 + lax.axis_index("core")

    image = (kinds == 1).astype(jnp.float32)
    text = (kinds == 2).astype(jnp.float32)
    counts = jnp.concatenate(
        [jnp.full((piece, block // 4), jnp.sum(kind)) for kind in (image, text)], 1
    )
    own = gather_ring(jnp.concatenate([act_basis, grad_basis, split(counts)[None]], 0), "zh")
    other = swap(own[:, groups:-1], "zl", 1)

    grads_z = swap(after(grads, other), "zl", 1)
    grads_zc = swap(grads_z, "core", 1)

    counts = jnp.sum(join(own[:, -1]), axis=0)
    left = own[:, :3].reshape(12, piece, block)
    left = gather(jnp.concatenate([left, split(counts)[None]], 0), "x")
    counts = add_up(jnp.sum(join(left[:, -1]), axis=0), "y")
    grads_c = swap(after(grads, counts), "core", 1)
    left = gather(left[:, :-1], "y").reshape(4, 4, 4, 3, piece, block)
    right = gather_ring(gather_ring(jnp.concatenate([own[:, 3:-1], other], 1), "y"), "x")
    weights = image / (2.0 * counts[0, 0]) + text / (2.0 * counts[0, block // 4])

    factors = call(
        factor_kernel,
        like((4, 4, 4, 2 * groups, piece, block), f32),
        [VMEM, ANY, ANY],
        VMEM,
        [
            pltpu.VMEM((2, tokens, wide), bf16),
            pltpu.SemaphoreType.DMA((2,)),
        ],
        8 * tokens * block * block,
        8 * 2**20,
        weights[:, None], acts, grads,
    )
    factors = pack(factors)
    left, right = after(left, factors), after(right, factors)

    left = jnp.transpose(left, (3, 1, 2, 0, 4, 5)).reshape(3, block, block)
    right = jnp.transpose(right, (3, 0, 2, 1, 4, 5)).reshape(3, block, block)
    grad_blocks = jnp.concatenate([left[2:], right], 0)
    grad_blocks_c = swap(grad_blocks, "core", 1)

    row = weights[None, :]
    place = jnp.stack([mp ^ x, y]).astype(jnp.int32)
    own_squares, act_squares = call(
        own_kernel,
        [like((2, 4, 4, 64, tokens), bf16), like((tokens, wide), bf16)],
        [SMEM, VMEM, ANY, ANY, ANY, ANY, ANY],
        [VMEM, VMEM],
        [
            pltpu.VMEM((3, tokens, wide), bf16),
            pltpu.VMEM((6, block, block), bf16),
            pltpu.SemaphoreType.DMA((5,)),
        ],
        12 * tokens * block * block,
        14 * 2**20,
        place, row, grads, grads_z, grad_blocks, acts, left[:2],
    )
    messages = call(
        send_kernel,
        [like((2, 1024, 256), f32)] * 2
        + [like((4, 512, 256), f32)] * 2
        + [like((4, 4, 4, 64, tokens), bf16)],
        [SMEM, VMEM, ANY, ANY, ANY, ANY, ANY],
        [VMEM] * 4 + [ANY],
        [
            pltpu.VMEM((4, 4, 4, 64, tokens), bf16),
            pltpu.VMEM((tokens, wide), bf16),
            pltpu.VMEM((2, tokens, wide), bf16),
            pltpu.VMEM((4, block, block), bf16),
            pltpu.SemaphoreType.DMA((6,)),
        ],
        8 * tokens * block * block + 4 * tokens * wide * wide,
        24 * 2**20,
        place, row, own_squares, act_squares, grads_c, grads_zc, grad_blocks_c,
    )
    packed = [pack(m.reshape(1, -1, 256))[0] for m in messages[:4]]
    squares = after(messages[4], *packed)
    factors = deal(after(factors, *packed), "zh")
    kept = call(
        keep_kernel,
        [like((4, 256, 256), f32)] * 8,
        [ANY, ANY],
        [VMEM] * 8,
        [
            pltpu.VMEM((4, 4, 4, 64, tokens), bf16),
            pltpu.VMEM((tokens, wide), bf16),
            pltpu.SemaphoreType.DMA((2,)),
        ],
        4 * tokens * wide * wide,
        16 * 2**20,
        squares, act_squares,
    )

    halves = []
    for s in range(4):
        axis, other = (("x", "y"), ("y", "x"))[s // 2]
        first, second = ((1, 3), (3, 1))[s % 2]
        got = swap(packed[s], axis, first)
        scale = scale_of(got)
        got = got[:-16].reshape((2, 4, 256, 256) if s < 2 else (4, 2, 256, 256))
        near, far = (lax.index_in_dim(got, k ^ (s % 2), s // 2, False) for k in range(2))
        far = kept[2 * s + 1] + far.astype(f32) * scale
        total = kept[2 * s] + near.astype(f32) * scale + send(far, axis, second)
        got = swap(pack(jnp.concatenate([total[first], total[2]])[None])[0], other, first)
        scale = scale_of(got)
        near = total[0] + got[:256].astype(f32) * scale
        far = total[second] + got[256:512].astype(f32) * scale
        halves.append((near, far))

    factors = after(factors, *(far for near, far in halves[:3]))
    factors = jnp.sum(unpack(factors), axis=0)
    factors = pack(factors.reshape(16, 2 * groups, piece, block))

    streams = []
    for s, (near, far) in enumerate(halves):
        other, second = ("y", "x")[s // 2], (3, 1)[s % 2]
        if s == 3:
            far = after(far, factors)
        streams.append((near + send(far, other, second)).reshape(4, 64, 256))
    factors = jnp.sum(unpack(deal(factors, ("x", "y"))), axis=0)
    factors = factors.reshape(2 * groups, piece, block)
    eigenvalues = direct_sum(jnp.concatenate(streams, 2), 0, "zh")
    return factors[:groups], factors[groups:], eigenvalues


def solution(mesh):
    fine = Mesh(mesh.devices.reshape(4, 4, 4, 2, 2), ("x", "zh", "y", "zl", "core"))
    dp, mp = ("x", "zh", "y"), ("zl", "core")
    in_specs = (P(dp, mp), P(dp, mp), P(dp), P(mp, dp, None), P(mp, dp, None))
    out_specs = (P(mp, dp, None), P(mp, dp, None), P(dp, mp))
    return jax.shard_map(
        per_device, mesh=fine, in_specs=in_specs, out_specs=out_specs, check_vma=False
    )
```

```python
import jax
import jax.numpy as jnp
from jax import lax
from jax.experimental import pallas as pl
from jax.experimental.pallas import tpu as pltpu
from jax.sharding import Mesh, PartitionSpec as P

HALF = jnp.float16
TOP = 14.0


def swap(value, axis, bits):
    size = lax.axis_size(axis)
    return lax.ppermute(value, axis, [(i, i ^ bits) for i in range(size)])


def shift(value, axis, step):
    size = lax.axis_size(axis)
    return lax.ppermute(value, axis, [(i, (i + step) % size) for i in range(size)])


def add_up(value, axis):
    return value + shift(value, axis, 1) + shift(value, axis, 2) + shift(value, axis, 3)


def deal(value, axes):
    return lax.all_to_all(value, axes, 0, 0, tiled=True)


def gather(value, axes):
    count = lax.axis_size(axes)
    return deal(jnp.broadcast_to(value[None], (count,) + value.shape), axes)


def gather_ring(value, axis):
    one, two, three = (shift(value, axis, step) for step in (1, 2, 3))
    twice = jnp.stack([three, two, one, value, three, two, one])
    return lax.dynamic_slice_in_dim(twice, 3 - lax.axis_index(axis), 4, 0)


def pack(value):
    count, width = value.shape[0], value.shape[-1]
    rows = value.reshape(count, -1, width)
    largest = jnp.max(jnp.abs(rows), axis=(0, 1), keepdims=True)
    power = jnp.ceil(jnp.log2(jnp.maximum(largest, 1e-30)))
    scaled = (rows * jnp.exp2(TOP - power)).astype(HALF)
    extra = jnp.broadcast_to(power, (count, 16, width)).astype(HALF)
    return jnp.concatenate([scaled, extra], 1)


def pack_rows(rows):
    largest = jnp.max(jnp.abs(rows), axis=0, keepdims=True)
    power = jnp.ceil(jnp.log2(jnp.maximum(largest, 1e-30)))
    place = lax.broadcasted_iota(jnp.int32, rows.shape, 0)
    return jnp.where(place < rows.shape[0] - 16, rows * jnp.exp2(TOP - power), power).astype(HALF)


def unpack(got):
    scale = jnp.exp2(got[:, -16:-15].astype(jnp.float32) - TOP)
    return got[:, :-16].astype(jnp.float32) * scale


def send(value, axis, bits):
    return unpack(swap(pack(value[None])[0], axis, bits)[None]).reshape(value.shape)


def pick(value, dim, index):
    return lax.dynamic_index_in_dim(value, index, dim, keepdims=False)


def deal_sum(value, axes):
    return jnp.sum(unpack(deal(pack(value), axes)), axis=0).reshape(value.shape[1:])


def direct_sum(value, dim, axis):
    me = lax.axis_index(axis)
    part = lambda bits: pick(value, dim, me ^ bits)
    return part(0) + send(part(1), axis, 1) + send(part(2), axis, 2) + send(part(3), axis, 3)


def after(value, *others):
    return lax.optimization_barrier((value, *others))[0]


def split(total):
    high = jnp.floor(total * (1 / 256))
    return jnp.concatenate([high, total - 256 * high], 1).astype(jnp.bfloat16)


def join(halves):
    wide = halves.astype(jnp.float32)
    middle = wide.shape[-1] // 2
    return 256 * wide[..., :middle] + wide[..., middle:]


def squared(basis, values, weights):
    projected = lax.dot_general(
        basis, values, (((0,), (1,)), ((), ())), preferred_element_type=jnp.float32
    )
    return (weights * (projected * projected)).astype(jnp.bfloat16)


def store(ref, lead, half, y, rows):
    for position in range(8):
        high, low = position // 4, position % 4
        ref[lead, low ^ y, 2 * half + high] = rows[position * 64 : (position + 1) * 64]


def factor_kernel(weights, acts, grads, out, held, sems):
    copies = [pltpu.make_async_copy(v, held.at[i], sems.at[i]) for i, v in enumerate((acts, grads))]
    for copy in copies:
        copy.start()
    width = out.shape[-1]
    for i in range(2):
        copies[i].wait()
        for b in range(2):
            values = held[i, :, b * width : (b + 1) * width]
            weighted = (weights[...] * values).astype(jnp.bfloat16)
            gram = lax.dot_general(
                weighted, values, (((0,), (0,)), ((), ())), preferred_element_type=jnp.float32
            )
            for p in range(16):
                rows = gram[p * 32 : (p + 1) * 32].reshape(4, 8, width)
                out[p % 4, p // 4, :, 2 * i + b] = rows


def own_kernel(
    place, weights, grads, grads_z, left, right, acts, squares, act_squares, held, blocks, sems
):
    copies = [
        pltpu.make_async_copy(grads, held.at[0], sems.at[0]),
        pltpu.make_async_copy(left, blocks.at[pl.ds(0, 3)], sems.at[1]),
        pltpu.make_async_copy(right, blocks.at[pl.ds(3, 3)], sems.at[2]),
        pltpu.make_async_copy(grads_z, held.at[1], sems.at[3]),
        pltpu.make_async_copy(acts, held.at[2], sems.at[4]),
    ]
    for copy in copies:
        copy.start()
    width = left.shape[-1]
    for copy in copies[:3]:
        copy.wait()
    for j in range(2):
        if j == 1:
            copies[3].wait()
        for b in range(2):
            values = held[j, :, b * width : (b + 1) * width]
            store(squares, j, b, place[1], squared(blocks[2 + 2 * j + b], values, weights[...]))
    copies[4].wait()
    for b in range(2):
        projected = jnp.dot(
            held[2, :, b * width : (b + 1) * width],
            blocks[b],
            preferred_element_type=jnp.float32,
        )
        act_squares[:, b * width : (b + 1) * width] = (projected * projected).astype(jnp.bfloat16)


def product(squares, act_squares, lead, count, s, out):
    width = out.shape[-1]
    columns = act_squares[:, s * width : (s + 1) * width]
    steps, size = (count, 1024) if s < 2 else (4, 256 * count)

    def one(i, carry):
        rows = squares[lead + i] if s < 2 else squares[i, lead : lead + count]
        out[pl.ds(pl.multiple_of(i * size, size), size), :] = jnp.dot(
            rows.reshape(size, columns.shape[0]), columns, preferred_element_type=jnp.float32
        )
        return carry

    lax.fori_loop(0, steps, one, 0)


def send_kernel(
    place, weights, own, act, grads_c, grads_zc, left, right, m0, m1, m2, m3, out,
    squares, act_squares, held, blocks, sems,
):
    copies = [
        pltpu.make_async_copy(grads_c, held.at[0], sems.at[0]),
        pltpu.make_async_copy(left, blocks.at[pl.ds(0, 1)], sems.at[1]),
        pltpu.make_async_copy(right, blocks.at[pl.ds(1, 3)], sems.at[2]),
        pltpu.make_async_copy(grads_zc, held.at[1], sems.at[3]),
        pltpu.make_async_copy(own.at[0], squares.at[place[0]], sems.at[4]),
        pltpu.make_async_copy(own.at[1], squares.at[place[0] ^ 2], sems.at[5]),
        pltpu.make_async_copy(act, act_squares, sems.at[6]),
    ]
    for copy in copies:
        copy.start()
    width = left.shape[-1]
    for copy in copies[:3]:
        copy.wait()
    for j in range(2):
        if j == 1:
            copies[3].wait()
        for b in range(2):
            values = held[j, :, b * width : (b + 1) * width]
            rows = squared(blocks[2 * j + b], values, weights[...])
            store(squares, place[0] ^ (2 * j + 1), b, place[1], rows)
    for copy in copies[4:]:
        copy.wait()
    results = [pltpu.make_async_copy(squares, out, sems.at[0])]
    results[0].start()
    for s, part in enumerate((m0, m1, m2, m3)):
        product(squares, act_squares, 1 + s % 2, 2, s, part)
        part[2048:, :] = jnp.zeros((16, part.shape[1]), jnp.float32)
    for copy in results:
        copy.wait()


def keep_kernel(squares_in, act_in, *refs):
    outs, (squares, act_squares, sems) = refs[:8], refs[8:]
    first = pltpu.make_async_copy(squares_in, squares, sems.at[0])
    second = pltpu.make_async_copy(act_in, act_squares, sems.at[1])
    first.start()
    second.start()
    first.wait()
    second.wait()
    for s in range(4):
        for k, lead in enumerate((0, (3, 1)[s % 2])):
            product(squares, act_squares, lead, 1, s, outs[2 * s + k])


ANY = pl.BlockSpec(memory_space=pl.ANY)
SMEM = pl.BlockSpec(memory_space=pltpu.SMEM)
VMEM = pl.BlockSpec(memory_space=pltpu.VMEM)
HBM = pl.BlockSpec(memory_space=pltpu.HBM)


def call(kernel, outs, ins, out_specs, scratch, room, flops, bytes_accessed, *args):
    return pl.pallas_call(
        kernel,
        out_shape=outs,
        in_specs=ins,
        out_specs=out_specs,
        scratch_shapes=scratch,
        compiler_params=pltpu.CompilerParams(vmem_limit_bytes=room * 2**20),
        cost_estimate=pl.CostEstimate(
            flops=flops, bytes_accessed=bytes_accessed, transcendentals=0
        ),
    )(*args)


def per_device(acts, grads, kinds, act_basis, grad_basis):
    tokens = acts.shape[0]
    groups, piece, block = act_basis.shape
    wide = groups * block
    f32, bf16 = jnp.float32, jnp.bfloat16
    like = jax.ShapeDtypeStruct
    x, y, zl = (lax.axis_index(a) for a in ("x", "y", "zl"))
    mp = zl * 2 + lax.axis_index("core")

    image = (kinds == 1).astype(jnp.float32)
    text = (kinds == 2).astype(jnp.float32)
    counts = jnp.concatenate(
        [jnp.full((piece, block // 4), jnp.sum(kind)) for kind in (image, text)], 1
    )
    own = gather_ring(jnp.concatenate([act_basis, grad_basis, split(counts)[None]], 0), "zh")
    other = swap(own[:, groups:-1], "zl", 1)

    grads_z = swap(after(grads, other), "zl", 1)
    grads_zc = swap(grads_z, "core", 1)

    counts = jnp.sum(join(own[:, -1]), axis=0)
    left = own[:, :3].reshape(12, piece, block)
    left = gather(jnp.concatenate([left, split(counts)[None]], 0), "x")
    counts = add_up(jnp.sum(join(left[:, -1]), axis=0), "y")
    grads_c = swap(after(grads, counts), "core", 1)
    left = gather(left[:, :-1], "y").reshape(4, 4, 4, 3, piece, block)
    right = gather_ring(gather_ring(jnp.concatenate([own[:, 3:-1], other], 1), "y"), "x")
    weights = image / (2.0 * counts[0, 0]) + text / (2.0 * counts[0, block // 4])

    factors = call(
        factor_kernel,
        like((4, 4, 4, 2 * groups, piece, block), f32),
        [VMEM, ANY, ANY],
        VMEM,
        [
            pltpu.VMEM((2, tokens, wide), bf16),
            pltpu.SemaphoreType.DMA((2,)),
        ],
        18,
        8 * tokens * block * block,
        8 * 2**20,
        weights[:, None], acts, grads,
    )
    factors = pack(factors)
    left, right = after(left, factors), after(right, factors)

    left = jnp.transpose(left, (3, 1, 2, 0, 4, 5)).reshape(3, block, block)
    right = jnp.transpose(right, (3, 0, 2, 1, 4, 5)).reshape(3, block, block)
    left_c, right_c = swap(left[2:], "core", 1), swap(right, "core", 1)

    row = weights[None, :]
    place = jnp.stack([mp ^ x, y]).astype(jnp.int32)
    own_squares, act_squares = call(
        own_kernel,
        [like((2, 4, 4, 64, tokens), bf16), like((tokens, wide), bf16)],
        [SMEM, VMEM, ANY, ANY, ANY, ANY, ANY],
        [VMEM, VMEM],
        [
            pltpu.VMEM((3, tokens, wide), bf16),
            pltpu.VMEM((6, block, block), bf16),
            pltpu.SemaphoreType.DMA((5,)),
        ],
        20,
        12 * tokens * block * block,
        14 * 2**20,
        place, row, grads, grads_z, left, right, acts,
    )
    messages = call(
        send_kernel,
        [like((2064, 256), f32)] * 4 + [like((4, 4, 4, 64, tokens), bf16)],
        [SMEM, VMEM, ANY, ANY, ANY, ANY, ANY, ANY],
        [VMEM] * 4 + [HBM],
        [
            pltpu.VMEM((4, 4, 4, 64, tokens), bf16),
            pltpu.VMEM((tokens, wide), bf16),
            pltpu.VMEM((2, tokens, wide), bf16),
            pltpu.VMEM((4, block, block), bf16),
            pltpu.SemaphoreType.DMA((7,)),
        ],
        30,
        8 * tokens * block * block + 4 * tokens * wide * wide,
        24 * 2**20,
        place, row, own_squares, act_squares, grads_c, grads_zc, left_c, right_c,
    )
    packed = [pack_rows(m) for m in messages[:4]]
    squares = after(messages[4], *packed)
    factors = deal(after(factors, *packed), "zh")
    kept = call(
        keep_kernel,
        [like((1024, 256), f32)] * 8,
        [HBM, ANY],
        [VMEM] * 8,
        [
            pltpu.VMEM((4, 4, 4, 64, tokens), bf16),
            pltpu.VMEM((tokens, wide), bf16),
            pltpu.SemaphoreType.DMA((2,)),
        ],
        24,
        4 * tokens * wide * wide,
        16 * 2**20,
        squares, act_squares,
    )

    kept = [k.reshape(4, 256, 256) for k in kept]
    totals, middles, streams = [], [], []
    for s in range(4):
        axis, other = (("x", "y"), ("y", "x"))[s // 2]
        first, second = ((1, 3), (3, 1))[s % 2]
        got = unpack(swap(packed[s], axis, first)[None])
        got = got.reshape((2, 4, 256, 256) if s < 2 else (4, 2, 256, 256))
        near, far = (lax.index_in_dim(got, k ^ (s % 2), s // 2, False) for k in range(2))
        total = kept[2 * s] + near + send(kept[2 * s + 1] + far, axis, second)
        middles.append(send(jnp.stack([total[first], total[2]]), other, first))
        totals.append(total)
    for s, (total, middle) in enumerate(zip(totals, middles)):
        other, second = ("y", "x")[s // 2], (3, 1)[s % 2]
        total = total[0] + middle[0] + send(total[second] + middle[1], other, second)
        streams.append(total.reshape(4, 64, 256))
    eigenvalues = direct_sum(jnp.concatenate(streams, 2), 0, "zh")

    factors = jnp.sum(unpack(after(factors, *streams)), axis=0)
    factors = deal_sum(factors.reshape(16, 2 * groups, piece, block), ("x", "y"))
    return factors[:groups], factors[groups:], eigenvalues


def solution(mesh):
    fine = Mesh(mesh.devices.reshape(4, 4, 4, 2, 2), ("x", "zh", "y", "zl", "core"))
    dp, mp = ("x", "zh", "y"), ("zl", "core")
    in_specs = (P(dp, mp), P(dp, mp), P(dp), P(mp, dp, None), P(mp, dp, None))
    out_specs = (P(mp, dp, None), P(mp, dp, None), P(dp, mp))
    return jax.shard_map(
        per_device, mesh=fine, in_specs=in_specs, out_specs=out_specs, check_vma=False
    )
```

```python
import jax
import jax.numpy as jnp
from jax import lax
from jax.experimental import pallas as pl
from jax.experimental.pallas import tpu as pltpu
from jax.sharding import Mesh, PartitionSpec as P

HALF = jnp.float16
TOP = 14.0


def swap(value, axis, bits):
    size = lax.axis_size(axis)
    return lax.ppermute(value, axis, [(i, i ^ bits) for i in range(size)])


def shift(value, axis, step):
    size = lax.axis_size(axis)
    return lax.ppermute(value, axis, [(i, (i + step) % size) for i in range(size)])


def add_up(value, axis):
    return value + shift(value, axis, 1) + shift(value, axis, 2) + shift(value, axis, 3)


def deal(value, axes):
    return lax.all_to_all(value, axes, 0, 0, tiled=True)


def gather(value, axes):
    count = lax.axis_size(axes)
    return deal(jnp.broadcast_to(value[None], (count,) + value.shape), axes)


def gather_ring(value, axis):
    one, two, three = (shift(value, axis, step) for step in (1, 2, 3))
    twice = jnp.stack([three, two, one, value, three, two, one])
    return lax.dynamic_slice_in_dim(twice, 3 - lax.axis_index(axis), 4, 0)


def pack(value):
    count, width = value.shape[0], value.shape[-1]
    rows = value.reshape(count, -1, width)
    largest = jnp.max(jnp.abs(rows), axis=(0, 1), keepdims=True)
    power = jnp.ceil(jnp.log2(jnp.maximum(largest, 1e-30)))
    scaled = (rows * jnp.exp2(TOP - power)).astype(HALF)
    extra = jnp.broadcast_to(power, (count, 16, width)).astype(HALF)
    return jnp.concatenate([scaled, extra], 1)


def unpack(got):
    scale = jnp.exp2(got[:, -16:-15].astype(jnp.float32) - TOP)
    return got[:, :-16].astype(jnp.float32) * scale


def send(value, axis, bits):
    return unpack(swap(pack(value[None])[0], axis, bits)[None]).reshape(value.shape)


def pick(value, dim, index):
    return lax.dynamic_index_in_dim(value, index, dim, keepdims=False)


def deal_sum(value, axes):
    return jnp.sum(unpack(deal(pack(value), axes)), axis=0).reshape(value.shape[1:])


def direct_sum(value, dim, axis):
    me = lax.axis_index(axis)
    part = lambda bits: pick(value, dim, me ^ bits)
    return part(0) + send(part(1), axis, 1) + send(part(2), axis, 2) + send(part(3), axis, 3)


def ring_sum(part, axis, first):
    second = 4 - first
    got = send(jnp.stack([part(first), part(2)]), axis, first)
    return part(0) + got[0] + send(part(second) + got[1], axis, second)


def after(value, *others):
    return lax.optimization_barrier((value, *others))[0]


def split(total):
    high = jnp.floor(total * (1 / 256))
    return jnp.concatenate([high, total - 256 * high], 1).astype(jnp.bfloat16)


def join(halves):
    wide = halves.astype(jnp.float32)
    middle = wide.shape[-1] // 2
    return 256 * wide[..., :middle] + wide[..., middle:]


def squared(basis, values, weights):
    projected = lax.dot_general(
        basis, values, (((0,), (1,)), ((), ())), preferred_element_type=jnp.float32
    )
    return (weights * (projected * projected)).astype(jnp.bfloat16)


def store(ref, lead, half, y, rows):
    for position in range(8):
        high, low = position // 4, position % 4
        ref[lead, low ^ y, 2 * half + high] = rows[position * 64 : (position + 1) * 64]


def factor_kernel(weights, acts, grads, out, held, sems):
    copies = [pltpu.make_async_copy(v, held.at[i], sems.at[i]) for i, v in enumerate((acts, grads))]
    for copy in copies:
        copy.start()
    width = out.shape[-1]
    for i in range(2):
        copies[i].wait()
        for b in range(2):
            values = held[i, :, b * width : (b + 1) * width]
            weighted = (weights[...] * values).astype(jnp.bfloat16)
            gram = lax.dot_general(
                weighted, values, (((0,), (0,)), ((), ())), preferred_element_type=jnp.float32
            )
            for p in range(16):
                rows = gram[p * 32 : (p + 1) * 32].reshape(4, 8, width)
                out[p % 4, p // 4, :, 2 * i + b] = rows


def own_kernel(
    place, weights, grads, grads_z, basis, acts, act_basis, squares, act_squares, held, blocks, sems
):
    copies = [
        pltpu.make_async_copy(grads, held.at[0], sems.at[0]),
        pltpu.make_async_copy(basis, blocks.at[pl.ds(0, 4)], sems.at[1]),
        pltpu.make_async_copy(grads_z, held.at[1], sems.at[2]),
        pltpu.make_async_copy(act_basis, blocks.at[pl.ds(4, 2)], sems.at[3]),
        pltpu.make_async_copy(acts, held.at[2], sems.at[4]),
    ]
    for copy in copies:
        copy.start()
    width = basis.shape[-1]
    copies[0].wait()
    copies[1].wait()
    for j in range(2):
        if j == 1:
            copies[2].wait()
        for b in range(2):
            values = held[j, :, b * width : (b + 1) * width]
            store(squares, j, b, place[1], squared(blocks[2 * j + b], values, weights[...]))
    copies[3].wait()
    copies[4].wait()
    for b in range(2):
        projected = jnp.dot(
            held[2, :, b * width : (b + 1) * width],
            blocks[4 + b],
            preferred_element_type=jnp.float32,
        )
        act_squares[:, b * width : (b + 1) * width] = (projected * projected).astype(jnp.bfloat16)


def product(squares, act_squares, lead, s, out):
    width = out.shape[-1]
    columns = act_squares[:, s * width : (s + 1) * width]
    tokens = columns.shape[0]

    def one(i, carry):
        if s < 2:
            rows = squares[lead + i]
        else:
            rows = squares[i, lead : lead + out.shape[1] // 256]
        out[i] = jnp.dot(
            rows.reshape(-1, tokens), columns, preferred_element_type=jnp.float32
        )
        return carry

    lax.fori_loop(0, out.shape[0], one, 0)


def send_kernel(
    place, weights, own, act, grads_c, grads_zc, basis, m0, m1, m2, m3, out,
    squares, act_squares, held, blocks, sems,
):
    copies = [
        pltpu.make_async_copy(grads_c, held.at[0], sems.at[0]),
        pltpu.make_async_copy(basis, blocks, sems.at[1]),
        pltpu.make_async_copy(grads_zc, held.at[1], sems.at[2]),
        pltpu.make_async_copy(own.at[0], squares.at[place[0]], sems.at[3]),
        pltpu.make_async_copy(own.at[1], squares.at[place[0] ^ 2], sems.at[4]),
        pltpu.make_async_copy(act, act_squares, sems.at[5]),
    ]
    for copy in copies:
        copy.start()
    width = basis.shape[-1]
    copies[0].wait()
    copies[1].wait()
    for j in range(2):
        if j == 1:
            copies[2].wait()
        for b in range(2):
            values = held[j, :, b * width : (b + 1) * width]
            rows = squared(blocks[2 * j + b], values, weights[...])
            store(squares, place[0] ^ (2 * j + 1), b, place[1], rows)
    for copy in copies[3:]:
        copy.wait()
    results = [pltpu.make_async_copy(squares, out, sems.at[0])]
    results[0].start()
    for s, part in enumerate((m0, m1, m2, m3)):
        product(squares, act_squares, 1 + s % 2, s, part)
    for copy in results:
        copy.wait()


def keep_kernel(squares_in, act_in, *refs):
    outs, (squares, act_squares, sems) = refs[:8], refs[8:]
    first = pltpu.make_async_copy(squares_in, squares, sems.at[0])
    second = pltpu.make_async_copy(act_in, act_squares, sems.at[1])
    first.start()
    second.start()
    first.wait()
    second.wait()
    for s in range(4):
        for k, lead in enumerate((0, (3, 1)[s % 2])):
            part = outs[2 * s + k]
            product(squares, act_squares, lead, s, part if s >= 2 else part.reshape(1, 1024, 256))


ANY = pl.BlockSpec(memory_space=pl.ANY)
SMEM = pl.BlockSpec(memory_space=pltpu.SMEM)
VMEM = pl.BlockSpec(memory_space=pltpu.VMEM)


def call(kernel, outs, ins, out_specs, scratch, flops, bytes_accessed, *args):
    return pl.pallas_call(
        kernel,
        out_shape=outs,
        in_specs=ins,
        out_specs=out_specs,
        scratch_shapes=scratch,
        compiler_params=pltpu.CompilerParams(vmem_limit_bytes=44 * 2**20),
        cost_estimate=pl.CostEstimate(
            flops=flops, bytes_accessed=bytes_accessed, transcendentals=0
        ),
    )(*args)


def per_device(acts, grads, kinds, act_basis, grad_basis):
    tokens = acts.shape[0]
    groups, piece, block = act_basis.shape
    wide = groups * block
    f32, bf16 = jnp.float32, jnp.bfloat16
    like = jax.ShapeDtypeStruct
    x, y, zl = (lax.axis_index(a) for a in ("x", "y", "zl"))
    mp = zl * 2 + lax.axis_index("core")

    image = (kinds == 1).astype(jnp.float32)
    text = (kinds == 2).astype(jnp.float32)
    counts = jnp.concatenate(
        [jnp.full((piece, block // 4), jnp.sum(kind)) for kind in (image, text)], 1
    )
    own = gather_ring(jnp.concatenate([act_basis, grad_basis, split(counts)[None]], 0), "zh")
    other = swap(own[:, groups:-1], "zl", 1)

    grads_z = swap(after(grads, other), "zl", 1)
    grads_zc = swap(grads_z, "core", 1)

    counts = jnp.sum(join(own[:, -1]), axis=0)
    left = own[:, :3].reshape(12, piece, block)
    left = gather(jnp.concatenate([left, split(counts)[None]], 0), "x")
    counts = add_up(jnp.sum(join(left[:, -1]), axis=0), "y")
    grads_c = swap(after(grads, counts), "core", 1)
    left = gather(left[:, :-1], "y").reshape(4, 4, 4, 3, piece, block)
    right = gather_ring(gather_ring(jnp.concatenate([own[:, 3:-1], other], 1), "y"), "x")
    weights = image / (2.0 * counts[0, 0]) + text / (2.0 * counts[0, block // 4])

    factors = call(
        factor_kernel,
        like((4, 4, 4, 2 * groups, piece, block), f32),
        [VMEM, ANY, ANY],
        VMEM,
        [
            pltpu.VMEM((2, tokens, wide), bf16),
            pltpu.SemaphoreType.DMA((2,)),
        ],
        8 * tokens * block * block,
        8 * 2**20,
        weights[:, None], acts, grads,
    )
    factors = pack(factors)
    left, right = after(left, factors), after(right, factors)
    factors = deal(after(factors, grads_z), "zh")

    left = jnp.transpose(left, (3, 1, 2, 0, 4, 5)).reshape(3, block, block)
    right = jnp.transpose(right, (3, 0, 2, 1, 4, 5)).reshape(3, block, block)
    grad_blocks = jnp.concatenate([left[2:], right], 0)
    grad_blocks_c = swap(grad_blocks, "core", 1)

    row = weights[None, :]
    place = jnp.stack([mp ^ x, y]).astype(jnp.int32)
    own_squares, act_squares = call(
        own_kernel,
        [like((2, 4, 4, 64, tokens), bf16), like((tokens, wide), bf16)],
        [SMEM, VMEM, ANY, ANY, ANY, ANY, ANY],
        [VMEM, VMEM],
        [
            pltpu.VMEM((3, tokens, wide), bf16),
            pltpu.VMEM((6, block, block), bf16),
            pltpu.SemaphoreType.DMA((5,)),
        ],
        12 * tokens * block * block,
        14 * 2**20,
        place, row, grads, grads_z, grad_blocks, acts, left[:2],
    )
    messages = call(
        send_kernel,
        [like((2, 1024, 256), f32)] * 2
        + [like((4, 512, 256), f32)] * 2
        + [like((4, 4, 4, 64, tokens), bf16)],
        [SMEM, VMEM, ANY, ANY, ANY, ANY, ANY],
        [VMEM] * 4 + [ANY],
        [
            pltpu.VMEM((4, 4, 4, 64, tokens), bf16),
            pltpu.VMEM((tokens, wide), bf16),
            pltpu.VMEM((2, tokens, wide), bf16),
            pltpu.VMEM((4, block, block), bf16),
            pltpu.SemaphoreType.DMA((6,)),
        ],
        8 * tokens * block * block + 4 * tokens * wide * wide,
        24 * 2**20,
        place, row, own_squares, act_squares, grads_c, grads_zc, grad_blocks_c,
    )
    packed = [pack(m.reshape(1, -1, 256))[0] for m in messages[:4]]
    squares = after(messages[4], *packed)
    kept = call(
        keep_kernel,
        [like((4, 256, 256), f32)] * 8,
        [ANY, ANY],
        [VMEM] * 8,
        [
            pltpu.VMEM((4, 4, 4, 64, tokens), bf16),
            pltpu.VMEM((tokens, wide), bf16),
            pltpu.SemaphoreType.DMA((2,)),
        ],
        4 * tokens * wide * wide,
        16 * 2**20,
        squares, act_squares,
    )

    streams = []
    for s in range(4):
        axis, other = (("x", "y"), ("y", "x"))[s // 2]
        first = (1, 3)[s % 2]
        got = unpack(swap(packed[s], axis, first)[None])
        got = got.reshape((2, 4, 256, 256) if s < 2 else (4, 2, 256, 256))
        near, far = (lax.index_in_dim(got, k ^ (s % 2), s // 2, False) for k in range(2))
        total = kept[2 * s] + near + send(kept[2 * s + 1] + far, axis, 4 - first)
        streams.append(ring_sum(lambda bits: total[bits], other, first).reshape(4, 64, 256))
    eigenvalues = direct_sum(jnp.concatenate(streams, 2), 0, "zh")

    factors = jnp.sum(unpack(after(factors, streams[0])), axis=0)
    factors = deal_sum(factors.reshape(16, 2 * groups, piece, block), ("x", "y"))
    return factors[:groups], factors[groups:], eigenvalues


def solution(mesh):
    fine = Mesh(mesh.devices.reshape(4, 4, 4, 2, 2), ("x", "zh", "y", "zl", "core"))
    dp, mp = ("x", "zh", "y"), ("zl", "core")
    in_specs = (P(dp, mp), P(dp, mp), P(dp), P(mp, dp, None), P(mp, dp, None))
    out_specs = (P(mp, dp, None), P(mp, dp, None), P(dp, mp))
    return jax.shard_map(
        per_device, mesh=fine, in_specs=in_specs, out_specs=out_specs, check_vma=False
    )
```
